128 devices in a mesh: seq: 8 (over z, y_hi), head: 16 (over y_lo, x, core).
Axes of the slice: x: 4, y: 4 (y_hi: 2, y_lo: 2; y = y_hi * 2 + y_lo), z: 4, core: 2. Of those that a mesh axis runs over, the one named last changes fastest.
Arguments:
- video_q: bfloat16 [16384, 2048], P(('seq', 'head')), may hold values from -8 to 8
- video_k: bfloat16 [16384, 2048], P(('seq', 'head')), may hold values from -8 to 8
- video_v: bfloat16 [16384, 2048], P(('seq', 'head')), may hold values from -6 to 6
- video_cross_q: bfloat16 [16384, 2048], P(('seq', 'head')), may hold values from -8 to 8
- audio_q: bfloat16 [2048, 2048], P('seq', 'head'), may hold values from -8 to 8
- audio_k: bfloat16 [2048, 2048], P('seq', 'head'), may hold values from -8 to 8
- audio_v: bfloat16 [2048, 2048], P('seq', 'head'), may hold values from -6 to 6
- audio_cross_q: bfloat16 [2048, 2048], P('seq', 'head'), may hold values from -8 to 8
- out_weight: bfloat16 [2048, 3072], P('head'), may hold values from -0.125 to 0.125
Outputs:
- video_mixed: bfloat16 [16384, 3072], P(('seq', 'head'))
- audio_attn: bfloat16 [2048, 2048], P('seq', 'head')
The draws below stay inside these ranges and needn't reach their ends.
All inputs are finite; a program needn't handle non-finite values.
Results may differ from the reference program's by a relative error of at most 0.015.
Values may be sent and summed in bfloat16 or wider, within the bound.
No kernel may reach another device: no remote copies, remote signals or barrier semaphores. Data moves between devices by JAX's collectives and lax.ppermute only.
A program may use at most 128 MiB of HBM per device.

```python
import math
import jax
import jax.numpy as jnp
from jax import lax

D = 3072
HEADS = 16
HEAD_DIM = 128
TV = 16384
TA = 2048


def drawn_rows(key, row_count):
    return jnp.clip(1.8 * jax.random.normal(key, (row_count, HEADS * HEAD_DIM), jnp.float32), -8.0, 8.0)


def draw_video_q(key, part):
    key = jax.random.fold_in(key, 1)
    values = drawn_rows(key, TV)
    return values.astype(jnp.bfloat16)


def draw_video_k(key, part):
    key = jax.random.fold_in(key, 2)
    values = drawn_rows(key, TV)
    return values.astype(jnp.bfloat16)


def draw_video_cross_q(key, part):
    key = jax.random.fold_in(key, 3)
    values = drawn_rows(key, TV)
    return values.astype(jnp.bfloat16)


def draw_audio_q(key, part):
    key = jax.random.fold_in(key, 4)
    values = drawn_rows(key, TA)
    return values.astype(jnp.bfloat16)


def draw_audio_k(key, part):
    key = jax.random.fold_in(key, 5)
    values = drawn_rows(key, TA)
    return values.astype(jnp.bfloat16)


def draw_audio_cross_q(key, part):
    key = jax.random.fold_in(key, 6)
    values = drawn_rows(key, TA)
    return values.astype(jnp.bfloat16)


def block_scale(own_key, extent, cuts, smallest, largest):
    level, own = 1.0, jax.random.fold_in(own_key, 6)
    for dim, shards_of in cuts:
        heights = jnp.exp(jax.random.uniform(jax.random.fold_in(own, dim), (shards_of,), jnp.float32, smallest / len(cuts), largest / len(cuts)))
        level = level * jnp.repeat(heights, extent[dim] // shards_of).reshape([-1 if axis == dim else 1 for axis in range(len(extent))])
    return level


def gaussian(stream_key, extent, spread, most, pieces=(), kind=jnp.bfloat16):
    values = jax.random.normal(stream_key, extent, jnp.float32) * spread
    if len(pieces) > 0:
        values = block_scale(stream_key, extent, pieces, -0.22, 0.18) * values
    return jnp.clip(values, min=-most, max=most).astype(kind)


def setup_inputs(seed: int = 0) -> dict:
    seeds = jax.random.split(jax.random.key(seed), 10)
    return {
        "video_q": draw_video_q(jax.random.fold_in(seeds[9], 71), 0),
        "video_k": draw_video_k(jax.random.fold_in(seeds[9], 71), 0),
        "video_v": gaussian(seeds[2], (TV, HEADS * HEAD_DIM), 1.0, 6.0, ((0, 128),)),
        "video_cross_q": draw_video_cross_q(jax.random.fold_in(seeds[9], 71), 0),
        "audio_q": draw_audio_q(jax.random.fold_in(seeds[9], 71), 0),
        "audio_k": draw_audio_k(jax.random.fold_in(seeds[9], 71), 0),
        "audio_v": gaussian(seeds[6], (TA, HEADS * HEAD_DIM), 1.0, 6.0, ((0, 8), (1, 16))),
        "audio_cross_q": draw_audio_cross_q(jax.random.fold_in(seeds[9], 71), 0),
        "out_weight": gaussian(seeds[8], (HEADS * HEAD_DIM, D), (HEADS * HEAD_DIM) ** -0.5, 0.125, ((0, 16),)),
    }


def attention(queries, key_rows, value_rows):
    query_count = queries.shape[0]
    key_count = key_rows.shape[0]
    query_heads = queries.reshape(query_count, HEADS, HEAD_DIM).transpose(1, 0, 2)
    key_heads = key_rows.reshape(key_count, HEADS, HEAD_DIM).transpose(1, 0, 2)
    value_heads = value_rows.reshape(key_count, HEADS, HEAD_DIM).transpose(1, 0, 2)
    block_rows = math.gcd(query_count, 512)

    def one_head(triple):
        query_head, key_head, value_head = triple

        def one_block(query_block):
            scores = jnp.dot(query_block, key_head.T, preferred_element_type=jnp.float32) * (HEAD_DIM ** -0.5)
            row_max = jnp.max(scores, axis=1, keepdims=True)
            weights = jnp.exp(scores - row_max)
            rounded = weights.astype(jnp.bfloat16)
            summed = jnp.dot(rounded, value_head, preferred_element_type=jnp.float32)
            return summed / jnp.sum(weights, axis=1, keepdims=True)

        blocks = query_head.reshape(query_count // block_rows, block_rows, HEAD_DIM)
        return lax.map(one_block, blocks).reshape(query_count, HEAD_DIM)

    result = lax.map(one_head, (query_heads, key_heads, value_heads))
    return result.transpose(1, 0, 2).reshape(query_count, HEADS * HEAD_DIM)


def reference(video_q, video_k, video_v, video_cross_q, audio_q, audio_k, audio_v, audio_cross_q, out_weight):
    video_attn = (attention(video_q, video_k, video_v) + attention(video_cross_q, audio_k, audio_v)).astype(jnp.bfloat16)
    video_mixed = jnp.dot(video_attn, out_weight, preferred_element_type=jnp.float32).astype(jnp.bfloat16)
    audio_attn = (attention(audio_q, audio_k, audio_v) + attention(audio_cross_q, video_k, video_v)).astype(jnp.bfloat16)
    return video_mixed, audio_attn
```

```python
import jax
import jax.numpy as jnp
from jax import lax
from jax.experimental import pallas as pl
from jax.experimental.pallas import tpu as pltpu
from jax.sharding import Mesh, PartitionSpec as P

BF16 = jnp.bfloat16
F32 = jnp.float32
B = 128
HEADS = 16
SCORE_SCALE = B**-0.5 * 1.4426950408889634
LARGEST_SUM = 1e30
Q_BLOCKS = 18
STEP_BLOCKS = 6
STEP = STEP_BLOCKS * B
STEPS = Q_BLOCKS // STEP_BLOCKS
ROWS = B + 16
VMEM = 60 << 20


def params():
    return pltpu.CompilerParams(vmem_limit_bytes=VMEM)


def cost(flops, bytes_accessed):
    return pl.CostEstimate(flops=int(flops), bytes_accessed=int(bytes_accessed), transcendentals=0)


def pack_video_kernel(q_ref, k_ref, v_ref, x_ref, out_ref):
    for head in range(HEADS):
        columns = slice(head * B, head * B + B)
        out_ref[head, 0] = k_ref[:, columns]
        out_ref[head, 1] = v_ref[:, columns].T
        out_ref[head, 2] = q_ref[:, columns].T
        out_ref[head, 3] = x_ref[:, columns].T


def pack_video(q, k, v, x):
    return pl.pallas_call(
        pack_video_kernel,
        out_shape=jax.ShapeDtypeStruct((HEADS, 4, B, B), BF16),
        compiler_params=params(),
    )(q, k, v, x)


def pack_audio_kernel(q_ref, k_ref, v_ref, x_ref, out_ref):
    for block in range(2):
        rows = slice(block * B, block * B + B)
        out_ref[block, 0] = k_ref[rows, :]
        out_ref[block, 1] = v_ref[rows, :].T
        out_ref[block, 2] = x_ref[rows, :].T
        out_ref[block, 3] = q_ref[rows, :].T


def pack_audio(q, k, v, x):
    return pl.pallas_call(
        pack_audio_kernel,
        out_shape=jax.ShapeDtypeStruct((2, 4, B, B), BF16),
        compiler_params=params(),
    )(q, k, v, x)


def unpack_kernel(video_ref, audio_ref, a_ref, b_ref, q_ref):
    for piece, out_ref in enumerate((a_ref, b_ref)):
        out_ref[0:8] = video_ref[piece * 8 : piece * 8 + 8, 0:2]
        out_ref[8] = audio_ref[piece, 0:2]
    for kind in range(2):
        q_ref[kind, 0:16] = video_ref[:, 2 + kind]
        q_ref[kind, 16:18] = audio_ref[:, 2 + kind]


def unpack(video, audio):
    piece = jax.ShapeDtypeStruct((9, 2, B, B), BF16)
    return pl.pallas_call(
        unpack_kernel,
        out_shape=(piece, piece, jax.ShapeDtypeStruct((2, Q_BLOCKS, B, B), BF16)),
        compiler_params=params(),
    )(video, audio)


def lanes(blocks):
    return jnp.concatenate([blocks[index] for index in range(blocks.shape[0])], axis=1)


def scores_of(keys, queries):
    return jnp.dot(keys, queries, preferred_element_type=F32) * SCORE_SCALE


def attend_step(first, state, pieces, audio, queries):
    part = slice(8, 9) if audio else slice(0, 8)
    scores = [
        scores_of(ref[part, 0].reshape(-1, B), queries) for ref in pieces
    ]
    if first:
        shift = jnp.max(scores[0][: 2 * B], axis=0, keepdims=True)
        sums, values = jnp.zeros((8, STEP), F32), jnp.zeros((B, STEP), F32)
    else:
        values, sums, shift = state
    for ref, score in zip(pieces, scores):
        weights = jnp.exp2(score - shift)
        sums = sums + jnp.sum(weights.reshape(-1, 8, STEP), axis=0)
        values = values + jnp.dot(
            lanes(ref[part, 1]), weights.astype(BF16), preferred_element_type=F32
        )
    return values, sums, shift


def attend_step_careful(state, pieces, audio, queries):
    for ref in pieces:

        def body(block, state, ref=ref):
            values, sums, shift = state
            scores = scores_of(ref[block, 0], queries)
            newest = jnp.maximum(shift, jnp.max(scores, axis=0, keepdims=True))
            factor = jnp.exp2(shift - newest)
            weights = jnp.exp2(scores - newest)
            sums = sums * factor + jnp.sum(weights.reshape(-1, 8, STEP), axis=0)
            values = values * factor + jnp.dot(
                ref[block, 1], weights.astype(BF16), preferred_element_type=F32
            )
            return values, sums, newest

        state = lax.fori_loop(8, 9, body, state) if audio else lax.fori_loop(0, 8, body, state)
    return state


def stage_kernel(first, offset, *refs):
    if first:
        own_ref, other_ref, a_ref, b_ref, out_ref = refs
    else:
        own_ref, other_ref, a_ref, b_ref, in_ref, out_ref = refs
    step = pl.program_id(0) + offset
    for kind in range(2):
        own, other = lanes(own_ref[kind]), lanes(other_ref[kind])
        queries = jnp.where(step < STEPS, own, other)
        pieces = (a_ref, b_ref)
        if first:
            state = None
        else:
            state = (in_ref[kind, 0:B], in_ref[kind, B : B + 8], in_ref[kind, B + 8 : B + 9])
        values, sums, shift = attend_step(first, state, pieces, kind == 1, queries)
        safe = jnp.max(sums) < LARGEST_SUM

        @pl.when(safe)
        def _():
            out_ref[kind, 0:B] = values
            out_ref[kind, B : B + 8] = sums
            out_ref[kind, B + 8 : B + 16] = jnp.broadcast_to(shift, (8, STEP))

        @pl.when(jnp.logical_not(safe))
        def _():
            if first:
                again = (jnp.zeros((B, STEP), F32), jnp.zeros((8, STEP), F32), shift)
            else:
                again = (in_ref[kind, 0:B], in_ref[kind, B : B + 8], in_ref[kind, B + 8 : B + 9])
            new_values, new_sums, new_shift = attend_step_careful(
                again, pieces, kind == 1, queries
            )
            out_ref[kind, 0:B] = new_values
            out_ref[kind, B : B + 8] = new_sums
            out_ref[kind, B + 8 : B + 16] = jnp.broadcast_to(new_shift, (8, STEP))


def stage(own, other, a, b, state, offset, steps):
    first = state is None
    query_block = (2, STEP_BLOCKS, B, B)
    piece_spec = pl.BlockSpec((9, 2, B, B), lambda i: (0, 0, 0, 0))
    in_specs = [
        pl.BlockSpec(query_block, lambda i: (0, jnp.minimum(i + offset, STEPS - 1), 0, 0)),
        pl.BlockSpec(query_block, lambda i: (0, jnp.maximum(i + offset - STEPS, 0), 0, 0)),
        piece_spec,
        piece_spec,
    ]
    operands = [own, other, a, b]
    if not first:
        in_specs.append(pl.BlockSpec((2, ROWS, STEP), lambda i: (0, 0, i + offset)))
        operands.append(state)

    def kernel(*refs):
        stage_kernel(first, offset, *refs)

    return pl.pallas_call(
        kernel,
        grid=(steps,),
        in_specs=in_specs,
        out_specs=pl.BlockSpec((2, ROWS, STEP), lambda i: (0, 0, i)),
        out_shape=jax.ShapeDtypeStruct((2, ROWS, steps * STEP), F32),
        compiler_params=params(),
        cost_estimate=cost(steps * STEP * 18 * B * 4 * B * 3, 4 << 20),
    )(*operands)


def merge_kernel(own_ref, other_ref, video_ref, audio_ref):
    total = None
    for kind in range(2):
        shift_own, shift_other = own_ref[kind, B + 8 : B + 9], other_ref[kind, B + 8 : B + 9]
        largest = jnp.maximum(shift_own, shift_other)
        factor_own, factor_other = jnp.exp2(shift_own - largest), jnp.exp2(shift_other - largest)
        sums = (
            jnp.sum(own_ref[kind, B : B + 8], axis=0, keepdims=True) * factor_own
            + jnp.sum(other_ref[kind, B : B + 8], axis=0, keepdims=True) * factor_other
        )
        values = own_ref[kind, 0:B] * (factor_own / sums) + other_ref[kind, 0:B] * (
            factor_other / sums
        )
        total = values if total is None else total + values
    for block in range(STEP_BLOCKS):
        piece = total[:, block * B : block * B + B].T.astype(BF16)
        video_ref[block] = piece
        audio_ref[block] = piece


def merge(own, other):
    spec = pl.BlockSpec((2, ROWS, STEP), lambda i: (0, 0, i))
    return pl.pallas_call(
        merge_kernel,
        grid=(STEPS,),
        in_specs=[spec, spec],
        out_specs=(
            pl.BlockSpec((STEP_BLOCKS, B, B), lambda i: (i, 0, 0)),
            pl.BlockSpec((STEP_BLOCKS, B, B), lambda i: (0, 0, 0)),
        ),
        out_shape=(
            jax.ShapeDtypeStruct((Q_BLOCKS, B, B), BF16),
            jax.ShapeDtypeStruct((STEP_BLOCKS, B, B), BF16),
        ),
        compiler_params=params(),
        cost_estimate=cost(0, 6 << 20),
    )(own, other)


def project_kernel(rows_ref, weight_ref, out_ref):
    out_ref[...] = jnp.dot(
        lanes(rows_ref[...]), weight_ref[...], preferred_element_type=F32
    ).astype(BF16)


def project(rows, weight):
    width = weight.shape[1]
    tile = 512
    return pl.pallas_call(
        project_kernel,
        grid=(width // tile,),
        in_specs=[
            pl.BlockSpec((HEADS, B, B), lambda i: (0, 0, 0)),
            pl.BlockSpec((HEADS * B, tile), lambda i: (0, i)),
        ],
        out_specs=pl.BlockSpec((B, tile), lambda i: (0, i)),
        out_shape=jax.ShapeDtypeStruct((B, width), BF16),
        compiler_params=params(),
        cost_estimate=cost(2 * B * HEADS * B * width, HEADS * B * width * 2),
    )(rows, weight)


def local(
    video_q, video_k, video_v, video_cross_q, audio_q, audio_k, audio_v, audio_cross_q, out_weight
):
    plane = ("yl", "x", "yh")
    trade = [
        (z * 4 + yh * 2 + core, z * 4 + core * 2 + yh)
        for z in range(4)
        for yh in range(2)
        for core in range(2)
    ]
    up = [(z, (z + 1) % 4) for z in range(4)]
    down = [(z, (z + 3) % 4) for z in range(4)]
    swap = [(0, 1), (1, 0)]

    weight = lax.all_gather(out_weight, ("yl", "x", "c"), axis=0, tiled=True)
    audio = lax.ppermute(
        pack_audio(audio_q, audio_k, audio_v, audio_cross_q), ("z", "yh", "c"), trade
    )
    video = lax.all_to_all(
        pack_video(video_q, video_k, video_v, video_cross_q),
        plane,
        split_axis=0,
        concat_axis=0,
        tiled=True,
    )
    own_a, own_b, own_q = unpack(video, audio)
    other_q = lax.ppermute(own_q, "c", swap)
    up_a, down_a = lax.ppermute(own_a, "z", up), lax.ppermute(own_a, "z", down)
    up_b, down_b = lax.ppermute(own_b, "z", up), lax.ppermute(own_b, "z", down)
    far_a, far_b = lax.ppermute(up_a, "z", up), lax.ppermute(down_b, "z", down)

    state = stage(own_q, other_q, own_a, own_b, None, 0, 2 * STEPS)
    state = stage(own_q, other_q, up_a, down_a, state, 0, 2 * STEPS)
    state = stage(own_q, other_q, up_b, down_b, state, 0, 2 * STEPS)
    given = lax.ppermute(
        stage(own_q, other_q, far_a, far_b, state, STEPS, STEPS), "c", swap
    )
    kept = stage(own_q, other_q, far_a, far_b, state, 0, STEPS)
    video_attn, audio_tail = merge(kept, given)
    rows = lax.all_to_all(video_attn[:HEADS], plane, split_axis=0, concat_axis=0, tiled=True)
    video_mixed = project(rows, weight)
    audio_attn = lax.ppermute(
        audio_tail[STEP_BLOCKS - 2 :].reshape(2 * B, B), ("z", "yh", "c"), trade
    )
    return video_mixed, audio_attn


def solution(mesh):
    fine = Mesh(mesh.devices.reshape(4, 2, 2, 4, 2), ("z", "yh", "yl", "x", "c"))
    seq, head = ("z", "yh"), ("yl", "x", "c")
    tokens = P(seq + head, None)
    tower = P(seq, head)
    return jax.shard_map(
        local,
        mesh=fine,
        in_specs=(tokens,) * 4 + (tower,) * 4 + (P(head, None),),
        out_specs=(tokens, tower),
        check_vma=False,
    )
```

```python
import jax
import jax.numpy as jnp
from jax import lax
from jax.experimental import pallas as pl
from jax.experimental.pallas import tpu as pltpu
from jax.sharding import Mesh, PartitionSpec as P

BF16 = jnp.bfloat16
F32 = jnp.float32
B = 128
HEADS = 16
SCORE_SCALE = B**-0.5 * 1.4426950408889634
LARGEST_SUM = 1e30
Q_BLOCKS = 18
STEP_BLOCKS = 6
STEP = STEP_BLOCKS * B
STEPS = Q_BLOCKS // STEP_BLOCKS
ROWS = B + 16
VMEM = 24 << 20


def params():
    return pltpu.CompilerParams(vmem_limit_bytes=VMEM)


def cost(flops, bytes_accessed):
    return pl.CostEstimate(flops=int(flops), bytes_accessed=int(bytes_accessed), transcendentals=0)


def after(value, *others):
    return lax.optimization_barrier((value, *others))[0]


def pack_video_kernel(q_ref, k_ref, v_ref, x_ref, out_ref):
    for head in range(HEADS // 4):
        columns = slice(head * B, head * B + B)
        out_ref[head, 0] = k_ref[:, columns]
        out_ref[head, 1] = v_ref[:, columns].T
        out_ref[head, 2] = q_ref[:, columns].T
        out_ref[head, 3] = x_ref[:, columns].T


def pack_video(q, k, v, x):
    spec = pl.BlockSpec((B, 4 * B), lambda i: (0, i))
    return pl.pallas_call(
        pack_video_kernel,
        grid=(4,),
        in_specs=[spec] * 4,
        out_specs=pl.BlockSpec((4, 4, B, B), lambda i: (i, 0, 0, 0)),
        out_shape=jax.ShapeDtypeStruct((HEADS, 4, B, B), BF16),
        compiler_params=params(),
    )(q, k, v, x)


def pack_audio_kernel(q_ref, k_ref, v_ref, x_ref, keys_ref, queries_ref):
    for block in range(2):
        rows = slice(block * B, block * B + B)
        keys_ref[block, 0] = k_ref[rows, :]
        keys_ref[block, 1] = v_ref[rows, :].T
        queries_ref[0, block] = x_ref[rows, :].T
        queries_ref[1, block] = q_ref[rows, :].T


def pack_audio(q, k, v, x):
    shape = jax.ShapeDtypeStruct((2, 2, B, B), BF16)
    return pl.pallas_call(
        pack_audio_kernel,
        out_shape=(shape, shape),
        compiler_params=params(),
    )(q, k, v, x)


def unpack_kernel(video_ref, audio_ref, a_ref, b_ref, q_ref, x_ref):
    a_ref[...] = video_ref[0:8, 0:2]
    b_ref[...] = video_ref[8:16, 0:2]
    q_ref[0:16] = video_ref[:, 2]
    q_ref[16:18] = audio_ref[0]
    x_ref[0:16] = video_ref[:, 3]
    x_ref[16:18] = audio_ref[1]


def unpack(video, audio):
    piece = jax.ShapeDtypeStruct((8, 2, B, B), BF16)
    queries = jax.ShapeDtypeStruct((Q_BLOCKS, B, B), BF16)
    return pl.pallas_call(
        unpack_kernel,
        out_shape=(piece, piece, queries, queries),
        compiler_params=params(),
        cost_estimate=cost(0, 5 << 20),
    )(video, audio)


def lanes(blocks):
    return jnp.concatenate([blocks[index] for index in range(blocks.shape[0])], axis=1)


def scores_of(keys, queries):
    return jnp.dot(keys, queries, preferred_element_type=F32) * SCORE_SCALE


def sums_of(weights):
    return jnp.sum(weights.reshape(-1, 8, STEP), axis=0)


def attend_careful(state, pieces, queries):
    for ref in pieces:

        def body(block, state, ref=ref):
            values, sums, shift = state
            scores = scores_of(ref[block, 0], queries)
            newest = jnp.maximum(shift, jnp.max(scores, axis=0, keepdims=True))
            factor = jnp.exp2(shift - newest)
            weights = jnp.exp2(scores - newest)
            values = values * factor + jnp.dot(
                ref[block, 1], weights.astype(BF16), preferred_element_type=F32
            )
            return values, sums * factor + sums_of(weights), newest

        state = lax.fori_loop(0, ref.shape[0], body, state)
    return state


def store_state(out_ref, state):
    values, sums, shift = state
    out_ref[0:B] = values
    out_ref[B : B + 8] = sums
    out_ref[B + 8 : B + 16] = jnp.broadcast_to(shift, (8, STEP))


def stage_kernel(sides, first, piece_count, *refs):
    query_refs, refs = refs[:sides], refs[sides:]
    pieces, refs = refs[:piece_count], refs[piece_count:]
    state_refs, out_ref = refs[:-1], refs[-1]
    if sides == 2:
        own = pl.program_id(0) < STEPS
        queries = jnp.where(own, lanes(query_refs[0][...]), lanes(query_refs[1][...]))
    else:
        queries = lanes(query_refs[0][...])

    def load(rows):
        if len(state_refs) == 2:
            return jnp.where(own, state_refs[0][rows], state_refs[1][rows])
        return state_refs[0][rows]

    scores = [scores_of(ref[:, 0].reshape(-1, B), queries) for ref in pieces]
    if first:
        shift = jnp.max(scores[0][: 2 * B], axis=0, keepdims=True)
        before = (jnp.zeros((B, STEP), F32), jnp.zeros((8, STEP), F32), shift)
    else:
        before = (load(slice(0, B)), load(slice(B, B + 8)), load(slice(B + 8, B + 9)))
    values, sums, shift = before
    for ref, score in zip(pieces, scores):
        weights = jnp.exp2(score - shift)
        sums = sums + sums_of(weights)
        values = values + jnp.dot(
            lanes(ref[:, 1]), weights.astype(BF16), preferred_element_type=F32
        )
    store_state(out_ref, (values, sums, shift))

    @pl.when(jnp.logical_not(jnp.max(sums) < LARGEST_SUM))
    def _():
        if first:
            start = (jnp.zeros((B, STEP), F32), jnp.zeros((8, STEP), F32), shift)
        else:
            start = (load(slice(0, B)), load(slice(B, B + 8)), load(slice(B + 8, B + 9)))
        store_state(out_ref, attend_careful(start, pieces, queries))


def stage(queries, pieces, states=(), offset=0):
    sides = len(queries)
    block = (STEP_BLOCKS, B, B)
    own_index = lambda i: jnp.minimum(i, STEPS - 1)
    other_index = lambda i: jnp.maximum(i - STEPS, 0)
    if sides == 2:
        in_specs = [
            pl.BlockSpec(block, lambda i: (own_index(i), 0, 0)),
            pl.BlockSpec(block, lambda i: (other_index(i), 0, 0)),
        ]
    else:
        in_specs = [pl.BlockSpec(block, lambda i: (i, 0, 0))]
    keys = 0
    for piece in pieces:
        in_specs.append(pl.BlockSpec(piece.shape, lambda i: (0, 0, 0, 0)))
        keys += piece.shape[0] * B
    if len(states) == 2:
        in_specs.append(pl.BlockSpec((ROWS, STEP), lambda i: (0, own_index(i))))
        in_specs.append(pl.BlockSpec((ROWS, STEP), lambda i: (0, other_index(i))))
    elif len(states) == 1:
        in_specs.append(pl.BlockSpec((ROWS, STEP), lambda i: (0, i + offset)))

    def kernel(*refs):
        stage_kernel(sides, len(states) == 0, len(pieces), *refs)

    width = sides * Q_BLOCKS * B
    return pl.pallas_call(
        kernel,
        grid=(sides * STEPS,),
        in_specs=in_specs,
        out_specs=pl.BlockSpec((ROWS, STEP), lambda i: (0, i)),
        out_shape=jax.ShapeDtypeStruct((ROWS, width), F32),
        compiler_params=params(),
        cost_estimate=cost(width * keys * 4 * B * 2.5, 4 << 20),
    )(*queries, *pieces, *states)


def merge_kernel(own_ref, other_ref, cross_ref, video_ref, audio_ref):
    shift_own, shift_other = own_ref[B + 8 : B + 9], other_ref[B + 8 : B + 9]
    largest = jnp.maximum(shift_own, shift_other)
    factor_own, factor_other = jnp.exp2(shift_own - largest), jnp.exp2(shift_other - largest)
    sums = (
        jnp.sum(own_ref[B : B + 8], axis=0, keepdims=True) * factor_own
        + jnp.sum(other_ref[B : B + 8], axis=0, keepdims=True) * factor_other
    )
    factor_own, factor_other = factor_own / sums, factor_other / sums
    factor_cross = 1.0 / jnp.sum(cross_ref[B : B + 8], axis=0, keepdims=True)
    for block in range(Q_BLOCKS):
        part = slice(block * B, block * B + B)
        total = (
            own_ref[0:B, part] * factor_own[:, part]
            + other_ref[0:B, part] * factor_other[:, part]
            + cross_ref[0:B, part] * factor_cross[:, part]
        ).T.astype(BF16)
        if block < HEADS:
            video_ref[block] = total
        else:
            audio_ref[block - HEADS] = total


def merge(own, other, cross):
    spec = pl.BlockSpec((ROWS, Q_BLOCKS * B), lambda i: (0, 0))
    return pl.pallas_call(
        merge_kernel,
        grid=(1,),
        in_specs=[spec] * 3,
        out_specs=(
            pl.BlockSpec((HEADS, B, B), lambda i: (0, 0, 0)),
            pl.BlockSpec((2, B, B), lambda i: (0, 0, 0)),
        ),
        out_shape=(
            jax.ShapeDtypeStruct((HEADS, B, B), BF16),
            jax.ShapeDtypeStruct((2, B, B), BF16),
        ),
        compiler_params=params(),
        cost_estimate=cost(0, 6 << 20),
    )(own, other, cross)


def project_kernel(rows_ref, weight_ref, out_ref):
    out_ref[...] = jnp.dot(
        lanes(rows_ref[...]), weight_ref[...], preferred_element_type=F32
    ).astype(BF16)


def project(rows, weight):
    half = weight.shape[2]
    tile = 512
    tiles = half // tile
    return pl.pallas_call(
        project_kernel,
        grid=(2 * tiles,),
        in_specs=[
            pl.BlockSpec((HEADS, B, B), lambda i: (0, 0, 0)),
            pl.BlockSpec((None, HEADS * B, tile), lambda i: (i // tiles, 0, i % tiles)),
        ],
        out_specs=pl.BlockSpec((B, tile), lambda i: (0, i)),
        out_shape=jax.ShapeDtypeStruct((B, 2 * half), BF16),
        compiler_params=params(),
        cost_estimate=cost(4 * B * HEADS * B * half, HEADS * B * half * 4),
    )(rows, weight)


def local(
    video_q, video_k, video_v, video_cross_q, audio_q, audio_k, audio_v, audio_cross_q, out_weight
):
    plane = ("yl", "x", "yh")

    def trade(value, distance):
        pairs = [
            (z * 4 + yh * 2 + core, (z + distance) % 4 * 4 + core * 2 + yh)
            for z in range(4)
            for yh in range(2)
            for core in range(2)
        ]
        return lax.ppermute(value, ("z", "yh", "c"), pairs)

    def up(value):
        return lax.ppermute(value, "z", [(z, (z + 1) % 4) for z in range(4)])

    def down(value):
        return lax.ppermute(value, "z", [(z, (z + 3) % 4) for z in range(4)])

    def swap(value):
        return lax.ppermute(value, "c", [(0, 1), (1, 0)])

    video = lax.all_to_all(
        pack_video(video_q, video_k, video_v, video_cross_q),
        plane,
        split_axis=0,
        concat_axis=0,
        tiled=True,
    )
    audio_pair, audio_queries = pack_audio(audio_q, audio_k, audio_v, audio_cross_q)
    audio_queries = trade(audio_queries, 0)
    audio_own = jnp.concatenate([trade(audio_pair, distance) for distance in range(4)], axis=0)
    audio_other = swap(audio_own)

    half = out_weight.shape[1] // 2
    columns = lax.dynamic_slice_in_dim(out_weight, lax.axis_index("yh") * half, half, 1)
    weight = lax.all_gather(
        after(columns, video), ("yh", "yl", "x", "c"), axis=0, tiled=True
    ).reshape(2, HEADS * B, half)

    own_a, own_b, own_q, own_x = unpack(video, audio_queries)
    other_q = swap(own_q)
    up_a, down_b = up(own_a), down(own_b)
    own_state = stage([own_q], [own_a, own_b])
    up_b, down_a = up(after(own_b, own_state)), down(after(own_a, own_state))
    other_state = stage([other_q], [own_a, own_b])
    cross_state = stage([after(own_x, other_state)], [audio_own, audio_other])
    far_a, far_b = up(after(up_a, other_state)), down(after(down_b, other_state))
    state = stage([own_q, other_q], [up_a, down_b], [own_state, other_state])
    state = stage([own_q, other_q], [up_b, down_a], [state])
    given_state = stage([other_q], [far_a, far_b], [state], STEPS)
    given = swap(given_state)
    kept = stage([after(own_q, given_state)], [far_a, far_b], [state])
    video_attn, audio_attn = merge(kept, given, cross_state)
    rows = lax.all_to_all(video_attn, plane, split_axis=0, concat_axis=0, tiled=True)
    video_mixed = project(rows, weight)
    return video_mixed, trade(audio_attn.reshape(2 * B, B), 0)


def solution(mesh):
    fine = Mesh(mesh.devices.reshape(4, 2, 2, 4, 2), ("z", "yh", "yl", "x", "c"))
    seq, head = ("z", "yh"), ("yl", "x", "c")
    tokens = P(seq + head, None)
    tower = P(seq, head)
    return jax.shard_map(
        local,
        mesh=fine,
        in_specs=(tokens,) * 4 + (tower,) * 4 + (P(head, None),),
        out_specs=(tokens, tower),
        check_vma=False,
    )
```

```python
import jax
import jax.numpy as jnp
from jax import lax
from jax.experimental import pallas as pl
from jax.experimental.pallas import tpu as pltpu
from jax.sharding import Mesh, PartitionSpec as P

BF16 = jnp.bfloat16
F32 = jnp.float32
B = 128
HEADS = 16
SCORE_SCALE = B**-0.5 * 1.4426950408889634
LARGEST_SUM = 1e30
Q_BLOCKS = 18
STEP_BLOCKS = 6
STEP = STEP_BLOCKS * B
VIDEO = 8
STEPS = Q_BLOCKS // STEP_BLOCKS
ROWS = B + 16
VMEM = 24 << 20
PACK = 4
PROJECT_AHEAD = 8
PROJECT_ROWS = 512


def params():
    return pltpu.CompilerParams(vmem_limit_bytes=VMEM)


def cost(flops, bytes_accessed):
    return pl.CostEstimate(flops=int(flops), bytes_accessed=int(bytes_accessed), transcendentals=0)


def after(value, *others):
    return lax.optimization_barrier((value, *others))[0]


def pack_video_kernel(q_ref, k_ref, v_ref, x_ref, out_ref, rows, packed, in_semaphores, out_semaphores):
    pieces = HEADS // PACK
    ins, outs = [], []
    for piece in range(pieces):
        columns = pl.ds(piece * PACK * B, PACK * B)
        ins.append(
            [
                pltpu.make_async_copy(
                    ref.at[:, columns], rows.at[index, :, columns], in_semaphores.at[index, piece]
                )
                for index, ref in enumerate((k_ref, v_ref, q_ref, x_ref))
            ]
        )
        heads = pl.ds(piece * PACK, PACK)
        outs.append(
            pltpu.make_async_copy(packed.at[heads], out_ref.at[heads], out_semaphores.at[piece])
        )
        for copy in ins[piece]:
            copy.start()
    for piece in range(pieces):
        for copy in ins[piece]:
            copy.wait()
        for head in range(piece * PACK, (piece + 1) * PACK):
            columns = slice(head * B, head * B + B)
            packed[head, 0] = rows[0, :, columns]
            for index in range(1, 4):
                packed[head, index] = rows[index, :, columns].T
        outs[piece].start()
    for copy in outs:
        copy.wait()


def pack_video(q, k, v, x):
    pieces = HEADS // PACK
    any_space = pl.BlockSpec(memory_space=pl.ANY)
    return pl.pallas_call(
        pack_video_kernel,
        in_specs=[any_space] * 4,
        out_specs=any_space,
        out_shape=jax.ShapeDtypeStruct((HEADS, 4, B, B), BF16),
        scratch_shapes=[
            pltpu.VMEM((4, B, HEADS * B), BF16),
            pltpu.VMEM((HEADS, 4, B, B), BF16),
            pltpu.SemaphoreType.DMA((4, pieces)),
            pltpu.SemaphoreType.DMA((pieces,)),
        ],
        compiler_params=pltpu.CompilerParams(vmem_limit_bytes=62 << 20),
    )(q, k, v, x)


def pack_audio_kernel(q_ref, k_ref, v_ref, x_ref, out_ref):
    for block in range(2):
        rows = slice(block * B, block * B + B)
        out_ref[block, 0] = k_ref[rows, :]
        out_ref[block, 1] = v_ref[rows, :].T
        out_ref[block, 2] = x_ref[rows, :].T
        out_ref[block, 3] = q_ref[rows, :].T


def pack_audio(q, k, v, x):
    return pl.pallas_call(
        pack_audio_kernel,
        out_shape=jax.ShapeDtypeStruct((2, 4, B, B), BF16),
        compiler_params=params(),
    )(q, k, v, x)


def unpack_kernel(video_ref, audio_ref, a_ref, b_ref, q_ref, x_ref):
    for piece, out_ref in enumerate((a_ref, b_ref)):
        out_ref[0:VIDEO] = video_ref[piece * VIDEO : (piece + 1) * VIDEO, 0:2]
        out_ref[VIDEO] = audio_ref[piece, 0:2]
    for index, out_ref in enumerate((q_ref, x_ref)):
        out_ref[0:HEADS] = video_ref[:, 2 + index]
        out_ref[HEADS:Q_BLOCKS] = audio_ref[:, 2 + index]


def unpack(video, audio):
    piece = jax.ShapeDtypeStruct((VIDEO + 1, 2, B, B), BF16)
    queries = jax.ShapeDtypeStruct((Q_BLOCKS, B, B), BF16)
    return pl.pallas_call(
        unpack_kernel,
        out_shape=(piece, piece, queries, queries),
        compiler_params=params(),
        cost_estimate=cost(0, 5 << 20),
    )(video, audio)


def collect_kernel(*refs):
    for index, ref in enumerate(refs[:-1]):
        refs[-1][index] = ref[0]


def collect_audio(pieces):
    return pl.pallas_call(
        collect_kernel,
        grid=(1,),
        in_specs=[pl.BlockSpec((1, 2, B, B), lambda i: (VIDEO, 0, 0, 0))] * len(pieces),
        out_specs=pl.BlockSpec((len(pieces), 2, B, B), lambda i: (0, 0, 0, 0)),
        out_shape=jax.ShapeDtypeStruct((len(pieces), 2, B, B), BF16),
        compiler_params=params(),
        cost_estimate=cost(0, 1 << 20),
    )(*pieces)


def lanes(blocks):
    return jnp.concatenate([blocks[index] for index in range(blocks.shape[0])], axis=1)


def scores_of(keys, queries):
    return jnp.dot(keys, queries, preferred_element_type=F32) * SCORE_SCALE


def sums_of(weights):
    return jnp.sum(weights.reshape(-1, 8, STEP), axis=0)


def attend_careful(state, pieces, queries):
    for ref in pieces:

        def body(block, state, ref=ref):
            values, sums, shift = state
            scores = scores_of(ref[block, 0], queries)
            newest = jnp.maximum(shift, jnp.max(scores, axis=0, keepdims=True))
            factor = jnp.exp2(shift - newest)
            weights = jnp.exp2(scores - newest)
            values = values * factor + jnp.dot(
                ref[block, 1], weights.astype(BF16), preferred_element_type=F32
            )
            return values, sums * factor + sums_of(weights), newest

        state = lax.fori_loop(0, VIDEO, body, state)
    return state


def store_state(out_ref, state):
    values, sums, shift = state
    out_ref[0:B] = values
    out_ref[B : B + 8] = sums
    out_ref[B + 8 : B + 16] = jnp.broadcast_to(shift, (8, STEP))


def stage_kernel(sides, first, piece_count, *refs):
    query_refs, refs = refs[:sides], refs[sides:]
    pieces, refs = refs[:piece_count], refs[piece_count:]
    state_refs, out_ref = refs[:-1], refs[-1]
    if sides == 2:
        own = pl.program_id(0) < STEPS
        queries = jnp.where(own, lanes(query_refs[0][...]), lanes(query_refs[1][...]))
    else:
        queries = lanes(query_refs[0][...])

    def load(rows):
        if len(state_refs) == 2:
            return jnp.where(own, state_refs[0][rows], state_refs[1][rows])
        return state_refs[0][rows]

    scores = [scores_of(ref[0:VIDEO, 0].reshape(-1, B), queries) for ref in pieces]
    if first:
        shift = jnp.max(scores[0][: 2 * B], axis=0, keepdims=True)
        before = (jnp.zeros((B, STEP), F32), jnp.zeros((8, STEP), F32), shift)
    else:
        before = (load(slice(0, B)), load(slice(B, B + 8)), load(slice(B + 8, B + 9)))
    values, sums, shift = before
    for ref, score in zip(pieces, scores):
        weights = jnp.exp2(score - shift)
        sums = sums + sums_of(weights)
        values = values + jnp.dot(
            lanes(ref[0:VIDEO, 1]), weights.astype(BF16), preferred_element_type=F32
        )
    store_state(out_ref, (values, sums, shift))

    @pl.when(jnp.logical_not(jnp.max(sums) < LARGEST_SUM))
    def _():
        if first:
            start = (jnp.zeros((B, STEP), F32), jnp.zeros((8, STEP), F32), shift)
        else:
            start = (load(slice(0, B)), load(slice(B, B + 8)), load(slice(B + 8, B + 9)))
        store_state(out_ref, attend_careful(start, pieces, queries))


def stage(queries, pieces, states=(), offset=0):
    sides = len(queries)
    block = (STEP_BLOCKS, B, B)
    own_index = lambda i: jnp.minimum(i, STEPS - 1)
    other_index = lambda i: jnp.maximum(i - STEPS, 0)
    if sides == 2:
        in_specs = [
            pl.BlockSpec(block, lambda i: (own_index(i), 0, 0)),
            pl.BlockSpec(block, lambda i: (other_index(i), 0, 0)),
        ]
    else:
        in_specs = [pl.BlockSpec(block, lambda i: (i, 0, 0))]
    keys = 0
    for piece in pieces:
        in_specs.append(pl.BlockSpec(piece.shape, lambda i: (0, 0, 0, 0)))
        keys += VIDEO * B
    if len(states) == 2:
        in_specs.append(pl.BlockSpec((ROWS, STEP), lambda i: (0, own_index(i))))
        in_specs.append(pl.BlockSpec((ROWS, STEP), lambda i: (0, other_index(i))))
    elif len(states) == 1:
        in_specs.append(pl.BlockSpec((ROWS, STEP), lambda i: (0, i + offset)))

    def kernel(*refs):
        stage_kernel(sides, len(states) == 0, len(pieces), *refs)

    width = sides * Q_BLOCKS * B
    return pl.pallas_call(
        kernel,
        grid=(sides * STEPS,),
        in_specs=in_specs,
        out_specs=pl.BlockSpec((ROWS, STEP), lambda i: (0, i)),
        out_shape=jax.ShapeDtypeStruct((ROWS, width), F32),
        compiler_params=params(),
        cost_estimate=cost(width * keys * 4 * B * 2.5, 4 << 20),
    )(*queries, *pieces, *states)


def merge_kernel(own_ref, other_ref, cross_ref, video_ref, audio_ref):
    shift_own, shift_other = own_ref[B + 8 : B + 9], other_ref[B + 8 : B + 9]
    largest = jnp.maximum(shift_own, shift_other)
    factor_own, factor_other = jnp.exp2(shift_own - largest), jnp.exp2(shift_other - largest)
    sums = (
        jnp.sum(own_ref[B : B + 8], axis=0, keepdims=True) * factor_own
        + jnp.sum(other_ref[B : B + 8], axis=0, keepdims=True) * factor_other
    )
    factor_own, factor_other = factor_own / sums, factor_other / sums
    factor_cross = 1.0 / jnp.sum(cross_ref[B : B + 8], axis=0, keepdims=True)
    for block in range(Q_BLOCKS):
        part = slice(block * B, block * B + B)
        total = (
            own_ref[0:B, part] * factor_own[:, part]
            + other_ref[0:B, part] * factor_other[:, part]
            + cross_ref[0:B, part] * factor_cross[:, part]
        ).T.astype(BF16)
        if block < HEADS:
            video_ref[block] = total
        else:
            audio_ref[block - HEADS] = total


def merge(own, other, cross):
    spec = pl.BlockSpec((ROWS, Q_BLOCKS * B), lambda i: (0, 0))
    return pl.pallas_call(
        merge_kernel,
        grid=(1,),
        in_specs=[spec] * 3,
        out_specs=(
            pl.BlockSpec((HEADS, B, B), lambda i: (0, 0, 0)),
            pl.BlockSpec((2, B, B), lambda i: (0, 0, 0)),
        ),
        out_shape=(
            jax.ShapeDtypeStruct((HEADS, B, B), BF16),
            jax.ShapeDtypeStruct((2, B, B), BF16),
        ),
        compiler_params=params(),
        cost_estimate=cost(0, 6 << 20),
    )(own, other, cross)


def project_kernel(
    rows_ref, weight_ref, audio_in_ref, out_ref, audio_out_ref, buffer, total, semaphores
):
    audio_out_ref[...] = audio_in_ref[...]
    halves, depth, half = weight_ref.shape
    pieces = depth // PROJECT_ROWS
    copies = []
    for side in range(halves):
        for piece in range(pieces):
            rows = pl.ds(piece * PROJECT_ROWS, PROJECT_ROWS)
            copies.append(
                pltpu.make_async_copy(
                    weight_ref.at[side, rows],
                    buffer.at[side, rows],
                    semaphores.at[side * pieces + piece],
                )
            )
    for copy in copies[:PROJECT_AHEAD]:
        copy.start()
    for side in range(halves):
        columns = slice(side * half, side * half + half)
        for piece in range(pieces):
            now = side * pieces + piece
            copies[now].wait()
            if now + PROJECT_AHEAD < len(copies):
                copies[now + PROJECT_AHEAD].start()
            blocks = slice(piece * PROJECT_ROWS // B, (piece + 1) * PROJECT_ROWS // B)
            part = jnp.dot(
                lanes(rows_ref[blocks]),
                buffer[side, piece * PROJECT_ROWS : (piece + 1) * PROJECT_ROWS],
                preferred_element_type=F32,
            )
            if piece == 0:
                total[...] = part
            elif piece < pieces - 1:
                total[...] += part
            else:
                out_ref[:, columns] = (total[...] + part).astype(BF16)


def project(rows, weight, audio):
    halves, depth, half = weight.shape
    vmem = pl.BlockSpec(memory_space=pltpu.VMEM)
    return pl.pallas_call(
        project_kernel,
        in_specs=[vmem, pl.BlockSpec(memory_space=pl.ANY), vmem],
        out_specs=(vmem, vmem),
        out_shape=(
            jax.ShapeDtypeStruct((B, halves * half), BF16),
            jax.ShapeDtypeStruct((2 * B, B), BF16),
        ),
        scratch_shapes=[
            pltpu.VMEM(weight.shape, BF16),
            pltpu.VMEM((B, half), F32),
            pltpu.SemaphoreType.DMA((halves * depth // PROJECT_ROWS,)),
        ],
        compiler_params=pltpu.CompilerParams(vmem_limit_bytes=54 << 20),
        cost_estimate=cost(2 * B * depth * halves * half, depth * halves * half * 2),
    )(*(pltpu.with_memory_space_constraint(value, space) for value, space in ((rows, pltpu.VMEM), (weight, pltpu.HBM), (audio, pltpu.VMEM))))


def local(
    video_q, video_k, video_v, video_cross_q, audio_q, audio_k, audio_v, audio_cross_q, out_weight
):
    plane = ("yl", "x", "yh")

    def trade(value):
        pairs = [
            (z * 4 + yh * 2 + core, z * 4 + core * 2 + yh)
            for z in range(4)
            for yh in range(2)
            for core in range(2)
        ]
        return lax.ppermute(value, ("z", "yh", "c"), pairs)

    def up(value):
        return lax.ppermute(value, "z", [(z, (z + 1) % 4) for z in range(4)])

    def down(value):
        return lax.ppermute(value, "z", [(z, (z + 3) % 4) for z in range(4)])

    def swap(value):
        return lax.ppermute(value, "c", [(0, 1), (1, 0)])

    video = lax.all_to_all(
        pack_video(video_q, video_k, video_v, video_cross_q),
        plane,
        split_axis=0,
        concat_axis=0,
        tiled=True,
    )
    audio = trade(pack_audio(audio_q, audio_k, audio_v, audio_cross_q))
    own_a, own_b, own_q, own_x = unpack(video, audio)
    half = out_weight.shape[1] // 2
    columns = lax.dynamic_slice_in_dim(out_weight, lax.axis_index("yh") * half, half, 1)
    weight = lax.all_gather(
        after(columns, own_q), ("yh", "yl", "x", "c"), axis=0, tiled=True
    ).reshape(2, HEADS * B, half)

    other_q = swap(own_q)
    up_a, down_b = up(own_a), down(own_b)
    own_state = stage([own_q], [own_a, own_b])
    up_b, down_a = up(after(own_b, own_state)), down(after(own_a, own_state))
    other_state = stage([other_q], [own_a, own_b])
    far_a, far_b = up(after(up_a, other_state)), down(after(down_b, other_state))
    state = stage([own_q, other_q], [up_a, down_b], [own_state, other_state])
    state = stage([own_q, other_q], [up_b, down_a], [state])
    audio_own = collect_audio([own_a, own_b, up_a, up_b, down_a, down_b, far_a, far_b])
    audio_other = swap(audio_own)
    given_state = stage([other_q], [far_a, far_b], [state], STEPS)
    given = swap(given_state)
    cross_state = stage([after(own_x, given_state)], [audio_own, audio_other])
    kept = stage([after(own_q, given_state)], [far_a, far_b], [state])
    video_attn, audio_attn = merge(kept, given, cross_state)
    rows = lax.all_to_all(
        video_attn, plane, split_axis=0, concat_axis=0, tiled=True
    )
    return project(rows, weight, trade(audio_attn.reshape(2 * B, B)))


def solution(mesh):
    fine = Mesh(mesh.devices.reshape(4, 2, 2, 4, 2), ("z", "yh", "yl", "x", "c"))
    seq, head = ("z", "yh"), ("yl", "x", "c")
    tokens = P(seq + head, None)
    tower = P(seq, head)
    return jax.shard_map(
        local,
        mesh=fine,
        in_specs=(tokens,) * 4 + (tower,) * 4 + (P(head, None),),
        out_specs=(tokens, tower),
        check_vma=False,
    )
```

```python
import jax
import jax.numpy as jnp
from jax import lax
from jax.experimental import pallas as pl
from jax.experimental.pallas import tpu as pltpu
from jax.sharding import Mesh, PartitionSpec as P

BF16 = jnp.bfloat16
F32 = jnp.float32
B = 128
HEADS = 16
SCORE_SCALE = B**-0.5 * 1.4426950408889634
LARGEST_SUM = 1e30
Q_BLOCKS = 18
STEP_BLOCKS = 9
STEP = STEP_BLOCKS * B
VIDEO = 8
STEPS = Q_BLOCKS // STEP_BLOCKS
ROWS = B + 16
VMEM = 24 << 20
STAGE_COST = 0.6
PACK = 4
PROJECT_AHEAD = 8
PROJECT_ROWS = 512


def params():
    return pltpu.CompilerParams(vmem_limit_bytes=VMEM)


def cost(flops, bytes_accessed):
    return pl.CostEstimate(flops=int(flops), bytes_accessed=int(bytes_accessed), transcendentals=0)


def after(value, *others):
    return lax.optimization_barrier((value, *others))[0]


def pack_video_kernel(q_ref, k_ref, v_ref, x_ref, out_ref, rows, packed, in_semaphores, out_semaphores):
    pieces = HEADS // PACK
    ins, outs = [], []
    for piece in range(pieces):
        columns = pl.ds(piece * PACK * B, PACK * B)
        ins.append(
            [
                pltpu.make_async_copy(
                    ref.at[:, columns], rows.at[index, :, columns], in_semaphores.at[index, piece]
                )
                for index, ref in enumerate((k_ref, v_ref, q_ref, x_ref))
            ]
        )
        heads = pl.ds(piece * PACK, PACK)
        outs.append(
            pltpu.make_async_copy(packed.at[heads], out_ref.at[heads], out_semaphores.at[piece])
        )
        for copy in ins[piece]:
            copy.start()
    for piece in range(pieces):
        for copy in ins[piece]:
            copy.wait()
        for head in range(piece * PACK, (piece + 1) * PACK):
            columns = slice(head * B, head * B + B)
            packed[head, 0] = rows[0, :, columns]
            for index in range(1, 4):
                packed[head, index] = rows[index, :, columns].T
        outs[piece].start()
    for copy in outs:
        copy.wait()


def pack_video(q, k, v, x):
    pieces = HEADS // PACK
    any_space = pl.BlockSpec(memory_space=pl.ANY)
    return pl.pallas_call(
        pack_video_kernel,
        in_specs=[any_space] * 4,
        out_specs=any_space,
        out_shape=jax.ShapeDtypeStruct((HEADS, 4, B, B), BF16),
        scratch_shapes=[
            pltpu.VMEM((4, B, HEADS * B), BF16),
            pltpu.VMEM((HEADS, 4, B, B), BF16),
            pltpu.SemaphoreType.DMA((4, pieces)),
            pltpu.SemaphoreType.DMA((pieces,)),
        ],
        compiler_params=pltpu.CompilerParams(vmem_limit_bytes=62 << 20),
    )(q, k, v, x)


def pack_audio_kernel(q_ref, k_ref, v_ref, x_ref, out_ref):
    for block in range(2):
        rows = slice(block * B, block * B + B)
        out_ref[block, 0] = k_ref[rows, :]
        out_ref[block, 1] = v_ref[rows, :].T
        out_ref[block, 2] = x_ref[rows, :].T
        out_ref[block, 3] = q_ref[rows, :].T


def pack_audio(q, k, v, x):
    return pl.pallas_call(
        pack_audio_kernel,
        out_shape=jax.ShapeDtypeStruct((2, 4, B, B), BF16),
        compiler_params=params(),
    )(q, k, v, x)


def unpack_kernel(video_ref, audio_ref, a_ref, b_ref, audio_out_ref, q_ref, x_ref):
    a_ref[...] = video_ref[0:VIDEO, 0:2]
    b_ref[...] = video_ref[VIDEO : 2 * VIDEO, 0:2]
    audio_out_ref[...] = audio_ref[:, 0:2]
    for index, out_ref in enumerate((q_ref, x_ref)):
        out_ref[0:HEADS] = video_ref[:, 2 + index]
        out_ref[HEADS:Q_BLOCKS] = audio_ref[:, 2 + index]


def unpack(video, audio):
    def blocks(*shape):
        return jax.ShapeDtypeStruct((*shape, B, B), BF16)

    return pl.pallas_call(
        unpack_kernel,
        out_shape=(
            blocks(VIDEO, 2),
            blocks(VIDEO, 2),
            blocks(2, 2),
            blocks(Q_BLOCKS),
            blocks(Q_BLOCKS),
        ),
        compiler_params=params(),
        cost_estimate=cost(0, 5 << 20),
    )(video, audio)


def collect_kernel(*refs):
    for index, ref in enumerate(refs[:-1]):
        refs[-1][2 * index : 2 * index + 2] = ref[...]


def collect_audio(pieces):
    return pl.pallas_call(
        collect_kernel,
        out_shape=jax.ShapeDtypeStruct((2 * len(pieces), 2, B, B), BF16),
        compiler_params=params(),
        cost_estimate=cost(0, 1 << 20),
    )(*pieces)


def lanes(blocks):
    return jnp.concatenate([blocks[index] for index in range(blocks.shape[0])], axis=1)


def scores_of(keys, queries):
    return jnp.dot(keys, queries, preferred_element_type=F32) * SCORE_SCALE


def sums_of(weights):
    return jnp.sum(weights.reshape(-1, 8, STEP), axis=0)


def attend_careful(state, pieces, queries):
    for ref in pieces:

        def body(block, state, ref=ref):
            values, sums, shift = state
            scores = scores_of(ref[block, 0], queries)
            newest = jnp.maximum(shift, jnp.max(scores, axis=0, keepdims=True))
            factor = jnp.exp2(shift - newest)
            weights = jnp.exp2(scores - newest)
            values = values * factor + jnp.dot(
                ref[block, 1], weights.astype(BF16), preferred_element_type=F32
            )
            return values, sums * factor + sums_of(weights), newest

        state = lax.fori_loop(0, VIDEO, body, state)
    return state


def store_state(out_ref, state):
    values, sums, shift = state
    out_ref[0:B] = values
    out_ref[B : B + 8] = sums
    out_ref[B + 8 : B + 16] = jnp.broadcast_to(shift, (8, STEP))


def stage_kernel(sides, first, piece_count, *refs):
    query_refs, refs = refs[:sides], refs[sides:]
    pieces, refs = refs[:piece_count], refs[piece_count:]
    state_refs, out_ref = refs[:-1], refs[-1]
    if sides == 2:
        own = pl.program_id(0) < STEPS
        queries = jnp.where(own, lanes(query_refs[0][...]), lanes(query_refs[1][...]))
    else:
        queries = lanes(query_refs[0][...])

    def load(rows):
        if len(state_refs) == 2:
            return jnp.where(own, state_refs[0][rows], state_refs[1][rows])
        return state_refs[0][rows]

    scores = [scores_of(ref[0:VIDEO, 0].reshape(-1, B), queries) for ref in pieces]
    if first:
        shift = jnp.max(scores[0][: 2 * B], axis=0, keepdims=True)
        before = (jnp.zeros((B, STEP), F32), jnp.zeros((8, STEP), F32), shift)
    else:
        before = (load(slice(0, B)), load(slice(B, B + 8)), load(slice(B + 8, B + 9)))
    values, sums, shift = before
    for ref, score in zip(pieces, scores):
        weights = jnp.exp2(score - shift)
        sums = sums + sums_of(weights)
        values = values + jnp.dot(
            lanes(ref[0:VIDEO, 1]), weights.astype(BF16), preferred_element_type=F32
        )
    store_state(out_ref, (values, sums, shift))

    @pl.when(jnp.logical_not(jnp.max(sums) < LARGEST_SUM))
    def _():
        if first:
            start = (jnp.zeros((B, STEP), F32), jnp.zeros((8, STEP), F32), shift)
        else:
            start = (load(slice(0, B)), load(slice(B, B + 8)), load(slice(B + 8, B + 9)))
        store_state(out_ref, attend_careful(start, pieces, queries))


def stage(queries, pieces, states=(), offset=0):
    sides = len(queries)
    block = (STEP_BLOCKS, B, B)
    own_index = lambda i: jnp.minimum(i, STEPS - 1)
    other_index = lambda i: jnp.maximum(i - STEPS, 0)
    if sides == 2:
        in_specs = [
            pl.BlockSpec(block, lambda i: (own_index(i), 0, 0)),
            pl.BlockSpec(block, lambda i: (other_index(i), 0, 0)),
        ]
    else:
        in_specs = [pl.BlockSpec(block, lambda i: (i, 0, 0))]
    keys = 0
    for piece in pieces:
        in_specs.append(pl.BlockSpec(piece.shape, lambda i: (0, 0, 0, 0)))
        keys += VIDEO * B
    if len(states) == 2:
        in_specs.append(pl.BlockSpec((ROWS, STEP), lambda i: (0, own_index(i))))
        in_specs.append(pl.BlockSpec((ROWS, STEP), lambda i: (0, other_index(i))))
    elif len(states) == 1:
        in_specs.append(pl.BlockSpec((ROWS, STEP), lambda i: (0, i + offset)))

    def kernel(*refs):
        stage_kernel(sides, len(states) == 0, len(pieces), *refs)

    width = sides * Q_BLOCKS * B
    return pl.pallas_call(
        kernel,
        grid=(sides * STEPS,),
        in_specs=in_specs,
        out_specs=pl.BlockSpec((ROWS, STEP), lambda i: (0, i)),
        out_shape=jax.ShapeDtypeStruct((ROWS, width), F32),
        compiler_params=params(),
        cost_estimate=cost(width * keys * 4 * B * STAGE_COST, 1 << 20),
    )(*queries, *pieces, *states)


def merge_kernel(own_ref, other_ref, cross_ref, video_ref, audio_ref):
    shift_own, shift_other = own_ref[B + 8 : B + 9], other_ref[B + 8 : B + 9]
    largest = jnp.maximum(shift_own, shift_other)
    factor_own, factor_other = jnp.exp2(shift_own - largest), jnp.exp2(shift_other - largest)
    sums = (
        jnp.sum(own_ref[B : B + 8], axis=0, keepdims=True) * factor_own
        + jnp.sum(other_ref[B : B + 8], axis=0, keepdims=True) * factor_other
    )
    factor_own, factor_other = factor_own / sums, factor_other / sums
    factor_cross = 1.0 / jnp.sum(cross_ref[B : B + 8], axis=0, keepdims=True)
    for block in range(Q_BLOCKS):
        part = slice(block * B, block * B + B)
        total = (
            own_ref[0:B, part] * factor_own[:, part]
            + other_ref[0:B, part] * factor_other[:, part]
            + cross_ref[0:B, part] * factor_cross[:, part]
        ).T.astype(BF16)
        if block < HEADS:
            video_ref[block] = total
        else:
            audio_ref[block - HEADS] = total


def merge(own, other, cross):
    spec = pl.BlockSpec((ROWS, Q_BLOCKS * B), lambda i: (0, 0))
    return pl.pallas_call(
        merge_kernel,
        grid=(1,),
        in_specs=[spec] * 3,
        out_specs=(
            pl.BlockSpec((HEADS, B, B), lambda i: (0, 0, 0)),
            pl.BlockSpec((2, B, B), lambda i: (0, 0, 0)),
        ),
        out_shape=(
            jax.ShapeDtypeStruct((HEADS, B, B), BF16),
            jax.ShapeDtypeStruct((2, B, B), BF16),
        ),
        compiler_params=params(),
        cost_estimate=cost(0, 6 << 20),
    )(own, other, cross)


def project_kernel(
    rows_ref, weight_ref, audio_in_ref, out_ref, audio_out_ref, buffer, total, semaphores
):
    audio_out_ref[...] = audio_in_ref[...]
    halves, depth, half = weight_ref.shape
    pieces = depth // PROJECT_ROWS
    copies = []
    for side in range(halves):
        for piece in range(pieces):
            rows = pl.ds(piece * PROJECT_ROWS, PROJECT_ROWS)
            copies.append(
                pltpu.make_async_copy(
                    weight_ref.at[side, rows],
                    buffer.at[side, rows],
                    semaphores.at[side * pieces + piece],
                )
            )
    for copy in copies[:PROJECT_AHEAD]:
        copy.start()
    for side in range(halves):
        columns = slice(side * half, side * half + half)
        for piece in range(pieces):
            now = side * pieces + piece
            copies[now].wait()
            if now + PROJECT_AHEAD < len(copies):
                copies[now + PROJECT_AHEAD].start()
            blocks = slice(piece * PROJECT_ROWS // B, (piece + 1) * PROJECT_ROWS // B)
            part = jnp.dot(
                lanes(rows_ref[blocks]),
                buffer[side, piece * PROJECT_ROWS : (piece + 1) * PROJECT_ROWS],
                preferred_element_type=F32,
            )
            if piece == 0:
                total[...] = part
            elif piece < pieces - 1:
                total[...] += part
            else:
                out_ref[:, columns] = (total[...] + part).astype(BF16)


def project(rows, weight, audio):
    halves, depth, half = weight.shape
    vmem = pl.BlockSpec(memory_space=pltpu.VMEM)
    return pl.pallas_call(
        project_kernel,
        in_specs=[vmem, pl.BlockSpec(memory_space=pl.ANY), vmem],
        out_specs=(vmem, vmem),
        out_shape=(
            jax.ShapeDtypeStruct((B, halves * half), BF16),
            jax.ShapeDtypeStruct((2 * B, B), BF16),
        ),
        scratch_shapes=[
            pltpu.VMEM(weight.shape, BF16),
            pltpu.VMEM((B, half), F32),
            pltpu.SemaphoreType.DMA((halves * depth // PROJECT_ROWS,)),
        ],
        compiler_params=pltpu.CompilerParams(vmem_limit_bytes=54 << 20),
        cost_estimate=cost(2 * B * depth * halves * half, depth * halves * half * 2),
    )(*(pltpu.with_memory_space_constraint(value, space) for value, space in ((rows, pltpu.VMEM), (weight, pltpu.HBM), (audio, pltpu.VMEM))))


def local(
    video_q, video_k, video_v, video_cross_q, audio_q, audio_k, audio_v, audio_cross_q, out_weight
):
    plane = ("yl", "x", "yh")

    def trade(value):
        pairs = [
            (z * 4 + yh * 2 + core, z * 4 + core * 2 + yh)
            for z in range(4)
            for yh in range(2)
            for core in range(2)
        ]
        return lax.ppermute(value, ("z", "yh", "c"), pairs)

    def round_z(value, distance):
        return lax.ppermute(value, "z", [(z, (z + distance) % 4) for z in range(4)])

    def up(value):
        return round_z(value, 1)

    def down(value):
        return round_z(value, 3)

    def swap(value):
        return lax.ppermute(value, "c", [(0, 1), (1, 0)])

    video = lax.all_to_all(
        pack_video(video_q, video_k, video_v, video_cross_q),
        plane,
        split_axis=0,
        concat_axis=0,
        tiled=True,
    )
    audio = trade(pack_audio(audio_q, audio_k, audio_v, audio_cross_q))
    own_a, own_b, own_audio, own_q, own_x = unpack(video, audio)
    half = out_weight.shape[1] // 2
    columns = lax.dynamic_slice_in_dim(out_weight, lax.axis_index("yh") * half, half, 1)
    weight = lax.all_gather(
        after(columns, own_q), ("yh", "yl", "x", "c"), axis=0, tiled=True
    ).reshape(2, HEADS * B, half)

    other_q = swap(own_q)
    up_a, down_b = up(own_a), down(own_b)
    own_state = stage([own_q], [own_a, own_b])
    up_b, down_a = up(after(own_b, own_state)), down(after(own_a, own_state))
    other_state = stage([other_q], [own_a, own_b])
    far_a, far_b = up(after(up_a, other_state)), down(after(down_b, other_state))
    heard = [round_z(after(own_audio, own_state), distance) for distance in (1, 3, 2)]
    state = stage([own_q, other_q], [up_a, down_b], [own_state, other_state])
    audio_own = collect_audio([after(own_audio, state)] + heard)
    audio_other = swap(audio_own)
    state = stage([own_q, other_q], [up_b, down_a], [state])
    cross_state = stage([after(own_x, state)], [audio_own, audio_other])
    state = after(state, cross_state)
    given_state = stage([other_q], [far_a, far_b], [state], STEPS)
    given = swap(given_state)
    kept = stage([after(own_q, given_state)], [far_a, far_b], [state])
    video_attn, audio_attn = merge(kept, given, cross_state)
    rows = lax.all_to_all(
        video_attn, plane, split_axis=0, concat_axis=0, tiled=True
    )
    return project(rows, weight, trade(audio_attn.reshape(2 * B, B)))


def solution(mesh):
    fine = Mesh(mesh.devices.reshape(4, 2, 2, 4, 2), ("z", "yh", "yl", "x", "c"))
    seq, head = ("z", "yh"), ("yl", "x", "c")
    tokens = P(seq + head, None)
    tower = P(seq, head)
    return jax.shard_map(
        local,
        mesh=fine,
        in_specs=(tokens,) * 4 + (tower,) * 4 + (P(head, None),),
        out_specs=(tokens, tower),
        check_vma=False,
    )
```

```python
import jax
import jax.numpy as jnp
from jax import lax
from jax.experimental import pallas as pl
from jax.experimental.pallas import tpu as pltpu
from jax.sharding import Mesh, PartitionSpec as P

BF16 = jnp.bfloat16
F32 = jnp.float32
B = 128
HEADS = 16
SCORE_SCALE = B**-0.5 * 1.4426950408889634
LARGEST_SUM = 1e30
AUDIO = 2
Q_BLOCKS = 18
STEP_BLOCKS = 9
STEP = STEP_BLOCKS * B
VIDEO = 8
STEPS = Q_BLOCKS // STEP_BLOCKS
ROWS = B + 16
VMEM = 24 << 20
STAGE_COST = 0.6
PACK = 4
PROJECT_AHEAD = 8
PROJECT_ROWS = 512


def params():
    return pltpu.CompilerParams(vmem_limit_bytes=VMEM)


def cost(flops, bytes_accessed):
    return pl.CostEstimate(flops=int(flops), bytes_accessed=int(bytes_accessed), transcendentals=0)


def after(value, *others):
    return lax.optimization_barrier((value, *others))[0]


def pack_video_kernel(q_ref, k_ref, v_ref, x_ref, out_ref, rows, packed, in_semaphores, out_semaphores):
    pieces = HEADS // PACK
    ins, outs = [], []
    for piece in range(pieces):
        columns = pl.ds(piece * PACK * B, PACK * B)
        ins.append(
            [
                pltpu.make_async_copy(
                    ref.at[:, columns], rows.at[index, :, columns], in_semaphores.at[index, piece]
                )
                for index, ref in enumerate((k_ref, v_ref, q_ref, x_ref))
            ]
        )
        heads = pl.ds(piece * PACK, PACK)
        outs.append(
            pltpu.make_async_copy(packed.at[heads], out_ref.at[heads], out_semaphores.at[piece])
        )
        for copy in ins[piece]:
            copy.start()
    for piece in range(pieces):
        for copy in ins[piece]:
            copy.wait()
        for head in range(piece * PACK, (piece + 1) * PACK):
            columns = slice(head * B, head * B + B)
            packed[head, 0] = rows[0, :, columns]
            for index in range(1, 4):
                packed[head, index] = rows[index, :, columns].T
        outs[piece].start()
    for copy in outs:
        copy.wait()


def pack_video(q, k, v, x):
    pieces = HEADS // PACK
    any_space = pl.BlockSpec(memory_space=pl.ANY)
    return pl.pallas_call(
        pack_video_kernel,
        in_specs=[any_space] * 4,
        out_specs=any_space,
        out_shape=jax.ShapeDtypeStruct((HEADS, 4, B, B), BF16),
        scratch_shapes=[
            pltpu.VMEM((4, B, HEADS * B), BF16),
            pltpu.VMEM((HEADS, 4, B, B), BF16),
            pltpu.SemaphoreType.DMA((4, pieces)),
            pltpu.SemaphoreType.DMA((pieces,)),
        ],
        compiler_params=pltpu.CompilerParams(vmem_limit_bytes=62 << 20),
    )(q, k, v, x)


def pack_audio_kernel(q_ref, k_ref, v_ref, x_ref, out_ref):
    for block in range(2):
        rows = slice(block * B, block * B + B)
        out_ref[block, 0] = k_ref[rows, :]
        out_ref[block, 1] = v_ref[rows, :].T
        out_ref[block, 2] = x_ref[rows, :].T
        out_ref[block, 3] = q_ref[rows, :].T


def pack_audio(q, k, v, x):
    return pl.pallas_call(
        pack_audio_kernel,
        out_shape=jax.ShapeDtypeStruct((2, 4, B, B), BF16),
        compiler_params=params(),
    )(q, k, v, x)


def unpack_kernel(video_ref, audio_ref, a_ref, b_ref, audio_out_ref, q_ref, x_ref, semaphores):
    first, second = pl.ds(0, VIDEO), pl.ds(VIDEO, VIDEO)
    moves = (
        (video_ref.at[first, pl.ds(0, 2)], a_ref),
        (video_ref.at[second, pl.ds(0, 2)], b_ref),
        (video_ref.at[first, 2], q_ref.at[first]),
        (video_ref.at[second, 2], q_ref.at[second]),
        (video_ref.at[first, 3], x_ref.at[first]),
        (video_ref.at[second, 3], x_ref.at[second]),
    )
    copies = [
        pltpu.make_async_copy(source, target, semaphores.at[index])
        for index, (source, target) in enumerate(moves)
    ]
    for copy in copies:
        copy.start()
    audio_out_ref[...] = audio_ref[:, 0:2]
    q_ref[HEADS:Q_BLOCKS] = audio_ref[:, 2]
    x_ref[HEADS:Q_BLOCKS] = audio_ref[:, 3]
    for copy in copies:
        copy.wait()


def unpack(video, audio):
    def blocks(*shape):
        return jax.ShapeDtypeStruct((*shape, B, B), BF16)

    return pl.pallas_call(
        unpack_kernel,
        in_specs=[pl.BlockSpec(memory_space=pl.ANY), pl.BlockSpec(memory_space=pltpu.VMEM)],
        out_specs=(pl.BlockSpec(memory_space=pltpu.VMEM),) * 5,
        out_shape=(
            blocks(VIDEO, 2),
            blocks(VIDEO, 2),
            blocks(AUDIO, 2),
            blocks(Q_BLOCKS),
            blocks(Q_BLOCKS),
        ),
        scratch_shapes=[pltpu.SemaphoreType.DMA((6,))],
        compiler_params=params(),
        cost_estimate=cost(0, 5 << 20),
    )(pltpu.with_memory_space_constraint(video, pltpu.HBM), audio)


def collect_kernel(*refs):
    for index, ref in enumerate(refs[:-1]):
        refs[-1][2 * index : 2 * index + 2] = ref[...]


def collect_audio(pieces):
    return pl.pallas_call(
        collect_kernel,
        out_shape=jax.ShapeDtypeStruct((2 * len(pieces), 2, B, B), BF16),
        compiler_params=params(),
        cost_estimate=cost(0, 1 << 20),
    )(*pieces)


def lanes(blocks):
    return jnp.concatenate([blocks[index] for index in range(blocks.shape[0])], axis=1)


def scores_of(keys, queries):
    return jnp.dot(keys, queries, preferred_element_type=F32) * SCORE_SCALE


def sums_of(weights):
    return jnp.sum(weights.reshape(-1, 8, STEP), axis=0)


def attend_careful(state, pieces, queries):
    for ref in pieces:

        def body(block, state, ref=ref):
            values, sums, shift = state
            scores = scores_of(ref[block, 0], queries)
            newest = jnp.maximum(shift, jnp.max(scores, axis=0, keepdims=True))
            factor = jnp.exp2(shift - newest)
            weights = jnp.exp2(scores - newest)
            values = values * factor + jnp.dot(
                ref[block, 1], weights.astype(BF16), preferred_element_type=F32
            )
            return values, sums * factor + sums_of(weights), newest

        state = lax.fori_loop(0, VIDEO, body, state)
    return state


def store_state(out_ref, state):
    values, sums, shift = state
    out_ref[0:B] = values
    out_ref[B : B + 8] = sums
    out_ref[B + 8 : B + 16] = jnp.broadcast_to(shift, (8, STEP))


def stage_kernel(sides, first, piece_count, *refs):
    query_refs, refs = refs[:sides], refs[sides:]
    pieces, refs = refs[:piece_count], refs[piece_count:]
    state_refs, out_ref = refs[:-1], refs[-1]
    if sides == 2:
        own = pl.program_id(0) < STEPS
        queries = jnp.where(own, lanes(query_refs[0][...]), lanes(query_refs[1][...]))
    else:
        queries = lanes(query_refs[0][...])

    def load(rows):
        if len(state_refs) == 2:
            return jnp.where(own, state_refs[0][rows], state_refs[1][rows])
        return state_refs[0][rows]

    scores = [scores_of(ref[0:VIDEO, 0].reshape(-1, B), queries) for ref in pieces]
    if first:
        shift = jnp.max(scores[0][: 2 * B], axis=0, keepdims=True)
        before = (jnp.zeros((B, STEP), F32), jnp.zeros((8, STEP), F32), shift)
    else:
        before = (load(slice(0, B)), load(slice(B, B + 8)), load(slice(B + 8, B + 9)))
    values, sums, shift = before
    for ref, score in zip(pieces, scores):
        weights = jnp.exp2(score - shift)
        sums = sums + sums_of(weights)
        values = values + jnp.dot(
            lanes(ref[0:VIDEO, 1]), weights.astype(BF16), preferred_element_type=F32
        )
    store_state(out_ref, (values, sums, shift))

    @pl.when(jnp.logical_not(jnp.max(sums) < LARGEST_SUM))
    def _():
        if first:
            start = (jnp.zeros((B, STEP), F32), jnp.zeros((8, STEP), F32), shift)
        else:
            start = (load(slice(0, B)), load(slice(B, B + 8)), load(slice(B + 8, B + 9)))
        store_state(out_ref, attend_careful(start, pieces, queries))


def stage(queries, pieces, states=(), offset=0):
    sides = len(queries)
    block = (STEP_BLOCKS, B, B)
    own_index = lambda i: jnp.minimum(i, STEPS - 1)
    other_index = lambda i: jnp.maximum(i - STEPS, 0)
    if sides == 2:
        in_specs = [
            pl.BlockSpec(block, lambda i: (own_index(i), 0, 0)),
            pl.BlockSpec(block, lambda i: (other_index(i), 0, 0)),
        ]
    else:
        in_specs = [pl.BlockSpec(block, lambda i: (i, 0, 0))]
    keys = 0
    for piece in pieces:
        in_specs.append(pl.BlockSpec(piece.shape, lambda i: (0, 0, 0, 0)))
        keys += VIDEO * B
    if len(states) == 2:
        in_specs.append(pl.BlockSpec((ROWS, STEP), lambda i: (0, own_index(i))))
        in_specs.append(pl.BlockSpec((ROWS, STEP), lambda i: (0, other_index(i))))
    elif len(states) == 1:
        in_specs.append(pl.BlockSpec((ROWS, STEP), lambda i: (0, i + offset)))

    def kernel(*refs):
        stage_kernel(sides, len(states) == 0, len(pieces), *refs)

    width = sides * Q_BLOCKS * B
    return pl.pallas_call(
        kernel,
        grid=(sides * STEPS,),
        in_specs=in_specs,
        out_specs=pl.BlockSpec((ROWS, STEP), lambda i: (0, i)),
        out_shape=jax.ShapeDtypeStruct((ROWS, width), F32),
        compiler_params=params(),
        cost_estimate=cost(width * keys * 4 * B * STAGE_COST, 1 << 20),
    )(*queries, *pieces, *states)


def merge_kernel(own_ref, other_ref, cross_ref, video_ref, audio_ref):
    shift_own, shift_other = own_ref[B + 8 : B + 9], other_ref[B + 8 : B + 9]
    largest = jnp.maximum(shift_own, shift_other)
    factor_own, factor_other = jnp.exp2(shift_own - largest), jnp.exp2(shift_other - largest)
    sums = (
        jnp.sum(own_ref[B : B + 8], axis=0, keepdims=True) * factor_own
        + jnp.sum(other_ref[B : B + 8], axis=0, keepdims=True) * factor_other
    )
    factor_own, factor_other = factor_own / sums, factor_other / sums
    factor_cross = 1.0 / jnp.sum(cross_ref[B : B + 8], axis=0, keepdims=True)
    for block in range(Q_BLOCKS):
        part = slice(block * B, block * B + B)
        total = (
            own_ref[0:B, part] * factor_own[:, part]
            + other_ref[0:B, part] * factor_other[:, part]
            + cross_ref[0:B, part] * factor_cross[:, part]
        ).T.astype(BF16)
        if block < HEADS:
            video_ref[block] = total
        else:
            audio_ref[block - HEADS] = total


def merge(own, other, cross):
    spec = pl.BlockSpec((ROWS, Q_BLOCKS * B), lambda i: (0, 0))
    return pl.pallas_call(
        merge_kernel,
        grid=(1,),
        in_specs=[spec] * 3,
        out_specs=(
            pl.BlockSpec((HEADS, B, B), lambda i: (0, 0, 0)),
            pl.BlockSpec((2, B, B), lambda i: (0, 0, 0)),
        ),
        out_shape=(
            jax.ShapeDtypeStruct((HEADS, B, B), BF16),
            jax.ShapeDtypeStruct((2, B, B), BF16),
        ),
        compiler_params=params(),
        cost_estimate=cost(0, 6 << 20),
    )(own, other, cross)


def project_kernel(
    rows_ref, weight_ref, audio_in_ref, out_ref, audio_out_ref, buffer, total, semaphores
):
    audio_out_ref[...] = audio_in_ref[...]
    halves, depth, half = weight_ref.shape
    pieces = depth // PROJECT_ROWS
    copies = []
    for side in range(halves):
        for piece in range(pieces):
            rows = pl.ds(piece * PROJECT_ROWS, PROJECT_ROWS)
            copies.append(
                pltpu.make_async_copy(
                    weight_ref.at[side, rows],
                    buffer.at[side, rows],
                    semaphores.at[side * pieces + piece],
                )
            )
    for copy in copies[:PROJECT_AHEAD]:
        copy.start()
    for side in range(halves):
        columns = slice(side * half, side * half + half)
        for piece in range(pieces):
            now = side * pieces + piece
            copies[now].wait()
            if now + PROJECT_AHEAD < len(copies):
                copies[now + PROJECT_AHEAD].start()
            blocks = slice(piece * PROJECT_ROWS // B, (piece + 1) * PROJECT_ROWS // B)
            part = jnp.dot(
                lanes(rows_ref[blocks]),
                buffer[side, piece * PROJECT_ROWS : (piece + 1) * PROJECT_ROWS],
                preferred_element_type=F32,
            )
            if piece == 0:
                total[...] = part
            elif piece < pieces - 1:
                total[...] += part
            else:
                out_ref[:, columns] = (total[...] + part).astype(BF16)


def project(rows, weight, audio):
    halves, depth, half = weight.shape
    vmem = pl.BlockSpec(memory_space=pltpu.VMEM)
    return pl.pallas_call(
        project_kernel,
        in_specs=[vmem, pl.BlockSpec(memory_space=pl.ANY), vmem],
        out_specs=(vmem, vmem),
        out_shape=(
            jax.ShapeDtypeStruct((B, halves * half), BF16),
            jax.ShapeDtypeStruct((2 * B, B), BF16),
        ),
        scratch_shapes=[
            pltpu.VMEM(weight.shape, BF16),
            pltpu.VMEM((B, half), F32),
            pltpu.SemaphoreType.DMA((halves * depth // PROJECT_ROWS,)),
        ],
        compiler_params=pltpu.CompilerParams(vmem_limit_bytes=54 << 20),
        cost_estimate=cost(2 * B * depth * halves * half, depth * halves * half * 2),
    )(*(pltpu.with_memory_space_constraint(value, space) for value, space in ((rows, pltpu.VMEM), (weight, pltpu.HBM), (audio, pltpu.VMEM))))


def local(
    video_q, video_k, video_v, video_cross_q, audio_q, audio_k, audio_v, audio_cross_q, out_weight
):
    plane = ("yl", "x", "yh")

    def trade(value):
        pairs = [
            (z * 4 + yh * 2 + core, z * 4 + core * 2 + yh)
            for z in range(4)
            for yh in range(2)
            for core in range(2)
        ]
        return lax.ppermute(value, ("z", "yh", "c"), pairs)

    def round_z(value, distance):
        return lax.ppermute(value, "z", [(z, (z + distance) % 4) for z in range(4)])

    def up(value):
        return round_z(value, 1)

    def down(value):
        return round_z(value, 3)

    def swap(value):
        return lax.ppermute(value, "c", [(0, 1), (1, 0)])

    video = lax.all_to_all(
        pack_video(video_q, video_k, video_v, video_cross_q),
        plane,
        split_axis=0,
        concat_axis=0,
        tiled=True,
    )
    audio = trade(pack_audio(audio_q, audio_k, audio_v, audio_cross_q))
    own_a, own_b, own_audio, own_q, own_x = unpack(video, audio)
    half = out_weight.shape[1] // 2
    columns = lax.dynamic_slice_in_dim(out_weight, lax.axis_index("yh") * half, half, 1)
    weight = lax.all_gather(
        after(columns, own_q), ("yh", "yl", "x", "c"), axis=0, tiled=True
    ).reshape(2, HEADS * B, half)

    other_q = swap(own_q)
    up_a, down_b = up(own_a), down(own_b)
    own_state = stage([own_q], [own_a, own_b])
    up_b, down_a = up(after(own_b, own_state)), down(after(own_a, own_state))
    other_state = stage([other_q], [own_a, own_b])
    far_a, far_b = up(after(up_a, other_state)), down(after(down_b, other_state))
    heard = [round_z(after(own_audio, own_state), distance) for distance in (1, 3, 2)]
    state = stage([own_q, other_q], [up_a, down_b], [own_state, other_state])
    audio_own = collect_audio([after(own_audio, state)] + heard)
    audio_other = swap(audio_own)
    state = stage([own_q, other_q], [up_b, down_a], [state])
    cross_state = stage([after(own_x, state)], [audio_own, audio_other])
    state = after(state, cross_state)
    given_state = stage([other_q], [far_a, far_b], [state], STEPS)
    given = swap(given_state)
    kept = stage([after(own_q, given_state)], [far_a, far_b], [state])
    video_attn, audio_attn = merge(kept, given, cross_state)
    rows = lax.all_to_all(
        video_attn, plane, split_axis=0, concat_axis=0, tiled=True
    )
    return project(rows, weight, trade(audio_attn.reshape(2 * B, B)))


def solution(mesh):
    fine = Mesh(mesh.devices.reshape(4, 2, 2, 4, 2), ("z", "yh", "yl", "x", "c"))
    seq, head = ("z", "yh"), ("yl", "x", "c")
    tokens = P(seq + head, None)
    tower = P(seq, head)
    return jax.shard_map(
        local,
        mesh=fine,
        in_specs=(tokens,) * 4 + (tower,) * 4 + (P(head, None),),
        out_specs=(tokens, tower),
        check_vma=False,
    )
```
